32 devices in a mesh: blk: 4 (over x, core), sub: 4 (over z), rows: 2 (over y).
Axes of the slice: x: 2, y: 2, z: 4, core: 2. Of those that a mesh axis runs over, the one named last changes fastest.
Arguments:
- bem_matrix: bfloat16 [2, 4096, 32768], P(None, ('sub', 'rows'), 'blk'), may hold values from -0.0234375 to 0.0234375
- surface_field: bfloat16 [32768, 2, 128], P(('blk', 'sub', 'rows')), may hold values from -6 to 6
- owner: int32 [4096], P(('sub', 'rows')), may hold values from 0 to 7, as said below
- wet_offset: int32 [8], replicated, may hold values from 0 to 511
- wet_count: int32 [8], replicated, may hold values from 128 to 512
- coupling: float32 [8, 512, 512], P(('sub', 'rows')), may hold values from -0.25 to 0.25
Outputs:
- forces: float32 [8, 2, 128, 512], P(('sub', 'rows'), None, 'blk')
The draws below stay inside these ranges and needn't reach their ends.
Inputs may be any that keep to these rules, and one draw needn't show every extreme that they name: `owner`: in each aligned block of 512 rows (the rows of one index of sub and rows), no subdomain is named by more than 128 rows, and one subdomain is named by exactly 128 rows in every block.
All inputs are finite; a program needn't handle non-finite values.
Results may differ from the reference program's by a relative error of at most 0.0003.
Values may be sent and summed in bfloat16 or wider, within the bound.
A program may use at most 64 MiB of HBM per device.

```python
import jax
import jax.numpy as jnp
from jax import lax

ROWS_SR = 512
NV = 128
W = 512
S = 512
NC = 32768
NSUB = 8
R = 4096
CAP = 128


def draw_owner(key, part):
    key_hot = jax.random.fold_in(key, 11)
    key_blocks = jax.random.fold_in(key, 23)
    hottest = jax.random.randint(key_hot, (), 0, NSUB)

    def one_block(block_key):
        key_slots = jax.random.fold_in(block_key, 1)
        key_order = jax.random.fold_in(block_key, 2)
        chosen = jax.random.permutation(key_slots, (NSUB - 1) * CAP)[:ROWS_SR - CAP]
        others = chosen // CAP
        others = others + (others >= hottest).astype(others.dtype)
        listed = jnp.concatenate([jnp.full((CAP,), hottest, others.dtype), others])
        return jax.random.permutation(key_order, listed)
    block_keys = jax.random.split(key_blocks, R // ROWS_SR)
    return jax.vmap(one_block)(block_keys).reshape(R).astype(jnp.int32)


def with_ends(drawn, stream_key, low, high):
    longest = drawn.shape.index(max(drawn.shape))
    spots = []
    for shift in (0, 1):
        where = [jax.random.randint(jax.random.fold_in(stream_key, axis), (), 0, length) for axis, length in enumerate(drawn.shape)]
        where[longest] = (where[longest] + shift) % drawn.shape[longest]
        spots.append(tuple(where))
    return drawn.at[spots[0]].set(low).at[spots[1]].set(high)


def steps_of(rng, dims, shards, smallest, largest):
    loudness = 1.0
    for axis_at, blocks in shards:
        draws = jax.random.uniform(jax.random.fold_in(jax.random.fold_in(rng, 6), axis_at), (blocks,), jnp.float32, smallest / len(shards), largest / len(shards))
        loudness = loudness * jnp.repeat(jnp.exp(draws), dims[axis_at] // blocks).reshape((-1,) + (1,) * (len(dims) - 1 - axis_at))
    return loudness


def gaussian(rng, dims, spread, limit, cuts=(), kind=jnp.bfloat16):
    gain = steps_of(rng, dims, cuts, -0.22, 0.18) if cuts else 1.0
    entries = jax.random.normal(rng, dims, jnp.float32) * spread * gain
    return jnp.minimum(jnp.maximum(entries, -limit), limit).astype(kind)


def setup_inputs(seed: int = 0) -> dict:
    keys = jax.random.split(jax.random.key(seed), 7)
    bem_matrix = gaussian(keys[0], (2, R, NC), (2 * NC) ** -0.5, 0.0234375, ((1, 8), (2, 4)))
    surface_field = gaussian(keys[1], (NC, 2, NV), 1.0, 6.0, ((0, 32),))
    owner = draw_owner(jax.random.fold_in(keys[6], 71), 0)
    wet_offset = with_ends(jax.random.randint(keys[3], (NSUB,), 0, W), jax.random.fold_in(keys[3], 1), 0, W - 1).astype(jnp.int32)
    wet_count = with_ends(jax.random.randint(keys[4], (NSUB,), W // 4, W + 1), jax.random.fold_in(keys[4], 1), W // 4, W).astype(jnp.int32)
    coupling = gaussian(keys[5], (NSUB, W, S), W ** -0.5, 0.25, ((0, 8),), jnp.float32)
    return {"bem_matrix": bem_matrix, "surface_field": surface_field, "owner": owner, "wet_offset": wet_offset, "wet_count": wet_count, "coupling": coupling}


def reference(bem_matrix, surface_field, owner, wet_offset, wet_count, coupling):
    mixed = surface_field.reshape(NC, 2 * NV)
    nblocks = R // ROWS_SR
    zero_index = jnp.zeros((), jnp.int32)

    def block_product(index):
        start = (index * ROWS_SR).astype(jnp.int32)
        tile = lax.dynamic_slice(bem_matrix, (zero_index, start, zero_index), (2, ROWS_SR, NC))
        prod = jnp.dot(tile.reshape(2 * ROWS_SR, NC), mixed, preferred_element_type=jnp.float32)
        prod = prod.reshape(2, ROWS_SR, 2, NV)
        real_part = prod[0, :, 0] - prod[1, :, 1]
        imag_part = prod[1, :, 0] + prod[0, :, 1]
        return jnp.stack([real_part, imag_part], axis=1)

    pressure = lax.map(block_product, jnp.arange(nblocks, dtype=jnp.int32)).reshape(R, 2 * NV)
    onehot = (owner[:, None] == jnp.arange(NSUB, dtype=jnp.int32)[None, :]).astype(jnp.int32)
    earlier = jnp.cumsum(onehot, axis=0) - onehot
    rank = jnp.sum(earlier * onehot, axis=1).astype(jnp.int32)
    wet = rank < wet_count[owner]
    slot = ((wet_offset[owner] + rank) % W).astype(jnp.int32)
    contrib = jnp.where(wet[:, None], pressure, jnp.zeros_like(pressure))
    wet_block = jnp.zeros((NSUB, W, 2 * NV), jnp.float32).at[owner, slot].add(contrib)
    forces = jnp.einsum("owk,ows->oks", wet_block, coupling, precision=lax.Precision.HIGHEST)
    return forces.reshape(NSUB, 2, NV, S)
```

```python
import functools

import jax
import jax.numpy as jnp
from jax import lax
from jax.experimental import pallas as pl
from jax.experimental.pallas import tpu as pltpu
from jax.sharding import PartitionSpec as P

MESH = pl.DeviceIdType.MESH
BF = jnp.bfloat16
F32 = jnp.float32
HALVES = 2
NN = (((1,), (0,)), ((), ()))
NT = (((1,), (1,)), ((), ()))


def dot(a, b, dims):
    return lax.dot_general(a, b, dims, preferred_element_type=F32)


def split(x, parts):
    out = []
    for _ in range(parts):
        top = x.astype(BF)
        out.append(top)
        x = x - top.astype(F32)
    return out


def kernel(
    dims,
    a_ref, x_ref, owner_ref, off_ref, cnt_ref, coup_ref,
    out_ref,
    ab, xb, acc, rb, cb, st, gh, gl, pk, sb,
    a_sem, z_recv, e_recv, up_send, down_send, y_send, e_send,
    r_send, r_recv, c_send, c_recv, p_send, p_recv,
):
    nz, nb, vv, depth, cap = dims
    ns = 2 * nz
    rows = ab.shape[2]
    wet = coup_ref.shape[1]
    wide = xb.shape[2]
    half = wide // 2
    b, z, y = (lax.axis_index(name) for name in ("blk", "sub", "rows"))
    me = z * 2 + y
    pair = z + 1 - 2 * lax.rem(z, 2)

    barrier = pltpu.get_barrier_semaphore()
    peers = []
    for d in range(1, ns):
        other = lax.rem(me + d, ns)
        peers.append((b, other // 2, lax.rem(other, 2)))
    mates = [(lax.rem(b + d, nb), z, y) for d in range(1, nb)]
    for who in peers + mates:
        pl.semaphore_signal(barrier, inc=1, device_id=who, device_id_type=MESH)

    def a_copy(shard):
        return pltpu.make_async_copy(
            a_ref.at[:, :, pl.ds(pl.multiple_of(shard * depth, depth), depth)],
            ab.at[shard],
            a_sem.at[shard],
        )

    def near(k):
        if k == 0:
            return [(z, None)]
        return [(z - k, z - k >= 0), (z + k, z + k < nz)]

    def guarded(cond, body):
        if cond is None:
            body()
        else:
            pl.when(cond)(body)

    for k in range(nz):
        for zs, cond in near(k):

            def load(zs=zs):
                a_copy(zs * 2 + y).start()
                a_copy(zs * 2 + 1 - y).start()

            guarded(cond, load)

    pl.semaphore_wait(barrier, len(peers) + len(mates))

    def remote(src, dst, send, recv, who):
        return pltpu.make_async_remote_copy(
            src_ref=src, dst_ref=dst, send_sem=send, recv_sem=recv,
            device_id=who, device_id_type=MESH,
        )

    def up(h, zs):
        src = x_ref.at[h] if zs is z else xb.at[h, zs * 2 + y]
        return remote(src, xb.at[h, zs * 2 + y], up_send.at[h, zs], z_recv.at[h, zs * 2 + y], (b, z + 1, y))

    def down(h, zs):
        src = x_ref.at[h] if zs is z else xb.at[h, zs * 2 + y]
        return remote(src, xb.at[h, zs * 2 + y], down_send.at[h, zs], z_recv.at[h, zs * 2 + y], (b, z - 1, y))

    def across(h, zs):
        src = x_ref.at[h] if zs is z else xb.at[h, zs * 2 + y]
        return remote(src, xb.at[h, zs * 2 + y], y_send.at[h, zs], z_recv.at[h, zs * 2 + y], (b, z, 1 - y))

    def across_part(h):
        rows_ = pl.ds(0, half)
        slot = pair * 2 + y
        return remote(xb.at[h, slot, rows_], xb.at[h, slot, rows_], y_send.at[h, pair], z_recv.at[h, slot], (b, z, 1 - y))

    def extra(h):
        rows_ = pl.ds(half, half)
        slot = z * 2 + 1 - y
        return remote(xb.at[h, slot, rows_], xb.at[h, slot, rows_], e_send.at[h], e_recv.at[h], (b, pair, y))

    def arrived(h, slot):
        pltpu.make_async_copy(xb.at[h, slot], xb.at[h, slot], z_recv.at[h, slot]).wait()

    def arrived_pair(h):
        slot = pair * 2 + 1 - y
        low, high = pl.ds(0, half), pl.ds(half, half)
        pltpu.make_async_copy(xb.at[h, slot, low], xb.at[h, slot, low], z_recv.at[h, slot]).wait()
        pltpu.make_async_copy(xb.at[h, slot, high], xb.at[h, slot, high], e_recv.at[h]).wait()

    def start_own(h):
        across(h, z).start()
        pl.when(z < nz - 1)(lambda: up(h, z).start())
        pl.when(z > 0)(lambda: down(h, z).start())

    def multiply(h, shard, x, first=False):
        p = x.shape[0] // 2
        turned = jnp.concatenate([-x[p:], x[:p]], axis=0)
        total = dot(x, ab[shard, 0], NT) + dot(turned, ab[shard, 1], NT)
        total = total.reshape(2, nb, vv, rows)
        if first:
            acc[h] = total
        else:
            acc[h] += total

    start_own(0)

    owner = owner_ref[...]
    table = (lax.broadcasted_iota(jnp.int32, (ns, rows), 0) == owner).astype(F32)
    before_me = (
        lax.broadcasted_iota(jnp.int32, (rows, rows), 0)
        < lax.broadcasted_iota(jnp.int32, (rows, rows), 1)
    ).astype(F32).astype(BF)
    earlier = dot(table.astype(BF), before_me, NN)
    local_rank = jnp.sum(earlier * table, axis=0, keepdims=True).astype(jnp.int32)
    counts = jnp.sum(table, axis=1, keepdims=True)
    cb[me] = jnp.broadcast_to(counts, (ns, 128))
    count_copies = [
        remote(cb.at[me], cb.at[me], c_send.at[d], c_recv.at[d], who)
        for d, who in enumerate(peers)
    ]
    for c in count_copies:
        c.start()
    place = lax.broadcasted_iota(jnp.int32, (cap, rows), 0)
    for o in range(ns):
        st[o * cap : (o + 1) * cap] = (
            jnp.where((owner == o) & (local_rank == place), 1.0, 0.0).astype(BF)
        )

    def prepare():
        for d, c in enumerate(count_copies):
            c.wait_send()
            src = lax.rem(me + ns - 1 - d, ns)
            remote(cb.at[src], cb.at[src], c_send.at[d], c_recv.at[d], peers[d]).wait_recv()
        offset, limit = off_ref[me], cnt_ref[me]
        c_high, c_low = split(coup_ref[0], 2)
        mine = lax.broadcasted_iota(jnp.int32, (ns, 128), 0) == me
        at = lax.broadcasted_iota(jnp.int32, (cap, wet), 0)
        w = lax.broadcasted_iota(jnp.int32, (cap, wet), 1)
        before = jnp.zeros((1, wet), jnp.int32)
        for s in range(ns):
            here = jnp.sum(jnp.where(mine, cb[s], 0.0), axis=0, keepdims=True)
            here = jnp.concatenate([here] * (wet // 128), axis=1).astype(jnp.int32)
            rank = before + at
            slot = (rank + offset) & (wet - 1)
            hit = jnp.where((slot == w) & (rank < limit) & (at < here), 1.0, 0.0).astype(BF)
            gh[s * cap : (s + 1) * cap] = dot(hit, c_high, NN).astype(BF)
            gl[s * cap : (s + 1) * cap] = dot(hit, c_low, NN).astype(BF)
            before = before + here

    def reduce_copies(h):
        return [
            remote(acc.at[h, :, who[0]], rb.at[h, d], r_send.at[h, d], r_recv.at[h, d], who)
            for d, who in enumerate(mates)
        ]

    def regroup_copies(h):
        return [
            remote(pk.at[h, who[1] * 2 + who[2]], sb.at[h, me], p_send.at[h, d], p_recv.at[h, d], who)
            for d, who in enumerate(peers)
        ]

    def regroup(h):
        for c in reduce_copies(h):
            c.wait()
        mine = acc[h, :, b]
        for d in range(nb - 1):
            mine = mine + rb[h, d]
        mine = mine.reshape(2 * vv, rows)
        parts = jnp.concatenate(split(mine, 3), axis=0)
        n = 2 * vv
        moved = dot(parts, st[...], NT)
        moved = moved[:n] + moved[n : 2 * n] + moved[2 * n :]
        for o in range(ns):
            pk[h, o] = moved[:, o * cap : (o + 1) * cap]
        for c in regroup_copies(h):
            c.start()
        sb[h, me] = pk[h, me]

    def finish(h):
        for d, c in enumerate(regroup_copies(h)):
            c.wait_send()
            src = lax.rem(me + ns - 1 - d, ns)
            remote(pk.at[h, src], sb.at[h, src], p_send.at[h, d], p_recv.at[h, d], peers[d]).wait_recv()
        got = jnp.concatenate([sb[h, s] for s in range(ns)], axis=1)
        high, low = split(got, 2)
        n = 2 * vv
        both = dot(jnp.concatenate([high, low], axis=0), gh[...], NN)
        loads = both[:n] + both[n:] + dot(high, gl[...], NN)
        out_ref[0, :, h * vv : (h + 1) * vv, :] = loads.reshape(2, vv, loads.shape[1])

    def absorb(h, k):
        for zs, cond in near(k):

            def body(zs=zs):
                slot = zs * 2 + 1 - y
                if k == 1:
                    pl.when(zs == pair)(lambda: arrived_pair(h))
                    pl.when(zs != pair)(lambda: arrived(h, slot))
                else:
                    arrived(h, slot)
                    if k == 0:
                        extra(h).start()
                if h == 0:
                    a_copy(slot).wait()
                multiply(h, slot, xb[h, slot])

            guarded(cond, body)

    for h in range(HALVES):
        if h == 0:
            a_copy(me).wait()
        multiply(h, me, x_ref[h], first=True)
        for k in range(1, nz):
            for side, (zs, cond) in enumerate(near(k)):

                def body(zs=zs, side=side):
                    slot = zs * 2 + y
                    arrived(h, slot)
                    if side == 0:
                        pl.when(z < nz - 1)(lambda: up(h, zs).start())
                    else:
                        pl.when(z > 0)(lambda: down(h, zs).start())
                    if k == 1:
                        pl.when(zs == pair)(lambda: across_part(h).start())
                        pl.when(zs != pair)(lambda: across(h, zs).start())
                    else:
                        across(h, zs).start()

                guarded(cond, body)
            if k == nz - 1 and h + 1 < HALVES:
                start_own(h + 1)
            if k == 1:
                absorb(h, 0)
            for zs, cond in near(k):

                def body(zs=zs):
                    slot = zs * 2 + y
                    if h == 0:
                        a_copy(slot).wait()
                    multiply(h, slot, xb[h, slot])

                guarded(cond, body)
            if k == 1 and h == 0:
                prepare()
            if k == 1 and h > 0:
                regroup(h - 1)
            if k > 1:
                absorb(h, k - 1)
        absorb(h, nz - 1)
        for c in reduce_copies(h):
            c.start()
        if h > 0:
            finish(h - 1)
    regroup(HALVES - 1)
    for h in range(HALVES):
        extra(h).wait_send()
        for k in range(nz):
            for side, (zs, cond) in enumerate(near(k)):

                def body(zs=zs, side=side):
                    if side == 0:
                        pl.when(z < nz - 1)(lambda: up(h, zs).wait_send())
                    if side == 1 or k == 0:
                        pl.when(z > 0)(lambda: down(h, zs).wait_send())
                    if k == 1:
                        pl.when(zs == pair)(lambda: across_part(h).wait_send())
                        pl.when(zs != pair)(lambda: across(h, zs).wait_send())
                    else:
                        across(h, zs).wait_send()

                guarded(cond, body)
    finish(HALVES - 1)


def shards(bem_matrix, surface_field, owner, wet_offset, wet_count, coupling):
    _, rows, cols = bem_matrix.shape
    depth, _, vectors = surface_field.shape
    nz = lax.axis_size("sub")
    nb = lax.axis_size("blk")
    ns = 2 * nz
    vv = vectors // (nb * HALVES)
    cap = max(2 * rows // ns, 128)
    wide = 2 * nb * vv
    wet, loads = coupling.shape[1:]
    packed = surface_field.reshape(depth, 2, nb, HALVES, vv).transpose(3, 1, 2, 4, 0)
    packed = packed.reshape(HALVES, wide, depth)
    vmem = pl.BlockSpec(memory_space=pltpu.VMEM)
    smem = pl.BlockSpec(memory_space=pltpu.SMEM)
    dma = pltpu.SemaphoreType.DMA
    return pl.pallas_call(
        functools.partial(kernel, (nz, nb, vv, depth, cap)),
        out_shape=jax.ShapeDtypeStruct((1, 2, HALVES * vv, loads), F32),
        in_specs=[pl.BlockSpec(memory_space=pl.ANY), vmem, vmem, smem, smem, vmem],
        out_specs=vmem,
        scratch_shapes=[
            pltpu.VMEM((ns, 2, rows, depth), BF),
            pltpu.VMEM((HALVES, ns, wide, depth), BF),
            pltpu.VMEM((HALVES, 2, nb, vv, rows), F32),
            pltpu.VMEM((HALVES, nb - 1, 2, vv, rows), F32),
            pltpu.VMEM((ns, ns, 128), F32),
            pltpu.VMEM((ns * cap, rows), BF),
            pltpu.VMEM((ns * cap, loads), BF),
            pltpu.VMEM((ns * cap, loads), BF),
            pltpu.VMEM((HALVES, ns, 2 * vv, cap), F32),
            pltpu.VMEM((HALVES, ns, 2 * vv, cap), F32),
            dma((ns,)),
            dma((HALVES, ns)),
            dma((HALVES,)),
            dma((HALVES, nz)),
            dma((HALVES, nz)),
            dma((HALVES, nz)),
            dma((HALVES,)),
            dma((HALVES, nb - 1)),
            dma((HALVES, nb - 1)),
            dma((ns - 1,)),
            dma((ns - 1,)),
            dma((HALVES, ns - 1)),
            dma((HALVES, ns - 1)),
        ],
        compiler_params=pltpu.CompilerParams(
            collective_id=0, has_side_effects=True, vmem_limit_bytes=60 * 2**20
        ),
    )(bem_matrix, packed, owner.reshape(1, rows), wet_offset, wet_count, coupling)


def solution(mesh):
    return jax.shard_map(
        shards,
        mesh=mesh,
        in_specs=(
            P(None, ("sub", "rows"), "blk"),
            P(("blk", "sub", "rows"), None, None),
            P(("sub", "rows")),
            P(),
            P(),
            P(("sub", "rows"), None, None),
        ),
        out_specs=P(("sub", "rows"), None, "blk", None),
        check_vma=False,
    )
```
